32 devices in a mesh: obs: 4 (over y, x), unk: 8 (over z, core).
Axes of the slice: x: 2, y: 2, z: 4, core: 2. Of those that a mesh axis runs over, the one named last changes fastest.
Arguments:
- design: float32 [4096, 24576], P('obs', 'unk'), may hold values from -0.09375 to 0.09375
- weights: float32 [4096], P('obs'), may hold values from 0.25 to 4
Outputs:
- factor: float32 [24576, 1024], P(('unk', 'obs'))
The draws below stay inside these ranges and needn't reach their ends.
All inputs are finite; a program needn't handle non-finite values.
Results may differ from the reference program's by a relative error of at most 0.00011.
Values sent between devices are 32-bit elements; how exact they have to be, the bound alone decides.
A program may use at most 128 MiB of HBM per device.

```python
import math
import jax
import jax.numpy as jnp
from jax import lax

N = 24576
PANEL = 512
M = 4096


def steps_of(own_key, shape, cuts, least, top_value):
    loudness, own = 1.0, jax.random.fold_in(own_key, 6)
    for position, shards_of in cuts:
        draws = jnp.exp(jax.random.uniform(jax.random.fold_in(own, position), (shards_of,), jnp.float32, least / len(cuts), top_value / len(cuts)))
        loudness = loudness * jnp.repeat(draws, shape[position] // shards_of).reshape([-1 if axis == position else 1 for axis in range(len(shape))])
    return loudness


def noise(own_key, shape, scale, most, cuts=(), held_as=jnp.bfloat16):
    loudness = steps_of(own_key, shape, cuts, -0.22, 0.18) if cuts else 1.0
    values = jax.random.normal(own_key, shape, jnp.float32) * scale * loudness
    return jnp.minimum(jnp.maximum(values, -most), most).astype(held_as)


def setup_inputs(seed: int = 0) -> dict:
    key_list = jax.random.split(jax.random.key(seed), 3)
    return {
        "design": noise(key_list[0], (M, N), M ** -0.5, 0.09375, ((0, 4), (1, 8)), jnp.float32),
        "weights": jnp.clip(jnp.exp(math.log(4.0) - 2.7725887 * jax.random.uniform(key_list[1], (M,), jnp.float32) ** steps_of(key_list[1], (M,), ((0, 4),), -0.2, 0.2)), 0.25, 4.0),
    }


def reference(design, weights):
    panel_cols = design[:, :2 * PANEL]
    weighted = panel_cols * weights[:, None]
    gram = lax.dot_general(design.astype(jnp.float32), weighted.astype(jnp.float32), (((0,), (0,)), ((), ())), precision=lax.Precision.HIGHEST, preferred_element_type=jnp.float32)
    top_block = gram[:2 * PANEL]
    diag_factor = jnp.linalg.cholesky(top_block)
    return lax.linalg.triangular_solve(diag_factor, gram, left_side=False, lower=True, transpose_a=True)
```

```python
import functools
import jax
import jax.numpy as jnp
from jax import lax
from jax.experimental import pallas as pl
from jax.experimental.pallas import tpu as pltpu
from jax.sharding import PartitionSpec as P

PANEL = 512
BLOCK = 128
STRIP = 8


def split(value):
    high = value.astype(jnp.bfloat16)
    low = (value - high.astype(jnp.float32)).astype(jnp.bfloat16)
    return high, low


def dot_t(left, right):
    return lax.dot_general(
        left, right, (((0,), (0,)), ((), ())), preferred_element_type=jnp.float32
    )


def dot_3(left, right):
    left_high, left_low = split(left)
    right_high, right_low = split(right)
    dot = functools.partial(jnp.dot, preferred_element_type=jnp.float32)
    return dot(left_high, right_high) + dot(left_high, right_low) + dot(left_low, right_high)


def invert_factor(work):
    row = lax.broadcasted_iota(jnp.int32, (STRIP, 2 * BLOCK), 0)
    for strip in range(BLOCK // STRIP):
        start = strip * STRIP
        rows = work[start : start + STRIP, :]
        scale = jnp.zeros_like(rows)
        for step in range(STRIP):
            column = jnp.broadcast_to(
                rows[:, start + step : start + step + 1], (STRIP, 2 * BLOCK)
            )
            pivot = jnp.broadcast_to(column[step : step + 1, :], (STRIP, 2 * BLOCK))
            scale = jnp.where(row == step, pivot, scale)
            if step < STRIP - 1:
                pivot_row = jnp.broadcast_to(rows[step : step + 1, :], (STRIP, 2 * BLOCK))
                factor = jnp.where(row > step, column / pivot, 0.0)
                rows = rows - factor * pivot_row
        rows = rows * lax.rsqrt(scale)
        work[start : start + STRIP, :] = rows
        if start + STRIP < BLOCK:
            first = rows.astype(jnp.bfloat16).astype(jnp.float32)
            rest = rows - first
            second = rest.astype(jnp.bfloat16).astype(jnp.float32)
            third = rest - second
            right = jnp.concatenate([first, second, first, second, third, first], axis=0)
            left = jnp.concatenate([first, first, second, second, first, third], axis=0)
            update = dot_t(
                left[:, :BLOCK].astype(jnp.bfloat16), right.astype(jnp.bfloat16)
            )
            work[start + STRIP :, :] = work[start + STRIP :, :] - update[start + STRIP :, :]


def factor_kernel(both_ref, out_ref, done, work, block):
    width, total = both_ref.shape
    eye = (
        lax.broadcasted_iota(jnp.int32, (BLOCK, BLOCK), 0)
        == lax.broadcasted_iota(jnp.int32, (BLOCK, BLOCK), 1)
    ).astype(jnp.float32)

    def step(k, _):
        offset = pl.multiple_of(k * BLOCK, BLOCK)
        block[...] = both_ref[pl.ds(offset, BLOCK), :]

        def earlier(j, _):
            held = done[j, :, pl.ds(offset, BLOCK)]
            left = jnp.concatenate(
                [held[:BLOCK], held[2 * BLOCK :], held[BLOCK : 2 * BLOCK]], axis=0
            )
            block[...] = block[...] - dot_t(left, done[j])
            return 0

        lax.fori_loop(0, k, earlier, 0)
        work[:, :BLOCK] = block[:, pl.ds(offset, BLOCK)]
        work[:, BLOCK:] = eye
        invert_factor(work)
        column = dot_3(work[:, BLOCK:], block[...])
        high, low = split(column)
        done[k, :BLOCK, :] = high
        done[k, BLOCK : 2 * BLOCK, :] = low
        done[k, 2 * BLOCK :, :] = high
        out_ref[pl.ds(offset, BLOCK), :] = column[:, width:]
        return 0

    lax.fori_loop(0, width // BLOCK, step, 0)


def factor_rows(both):
    width, total = both.shape
    return pl.pallas_call(
        factor_kernel,
        out_shape=jax.ShapeDtypeStruct((width, total - width), jnp.float32),
        in_specs=[pl.BlockSpec(memory_space=pltpu.VMEM)],
        out_specs=pl.BlockSpec(memory_space=pltpu.VMEM),
        scratch_shapes=[
            pltpu.VMEM((width // BLOCK, 3 * BLOCK, total), jnp.bfloat16),
            pltpu.VMEM((BLOCK, 2 * BLOCK), jnp.float32),
            pltpu.VMEM((BLOCK, total), jnp.float32),
        ],
        compiler_params=pltpu.CompilerParams(vmem_limit_bytes=56 * 2**20),
    )(both)


def spread(block, axis, holder):
    block = jnp.where(lax.axis_index(axis) == holder, block, jnp.zeros_like(block))
    return lax.psum(block, axis)


def local(design, weights):
    panel_cols = spread(design[:, : 2 * PANEL], "unk", 0)
    weighted = panel_cols * weights[:, None]
    dot = functools.partial(
        lax.dot_general,
        dimension_numbers=(((0,), (0,)), ((), ())),
        precision=lax.Precision.HIGH,
        preferred_element_type=jnp.float32,
    )
    top_block = lax.psum(dot(weighted, panel_cols), "obs")
    partial_value = dot(weighted, design)
    owned = lax.psum_scatter(partial_value, "obs", scatter_dimension=1, tiled=True)
    return factor_rows(jnp.concatenate([top_block, owned], axis=1)).T


def solution(mesh):
    return jax.shard_map(
        local,
        mesh=mesh,
        in_specs=(P("obs", "unk"), P("obs")),
        out_specs=P(("unk", "obs"), None),
        check_vma=False,
    )
```

```python
import functools
import jax
import jax.numpy as jnp
from jax import lax
from jax.experimental import pallas as pl
from jax.experimental.pallas import tpu as pltpu
from jax.sharding import PartitionSpec as P

PANEL = 512
BLOCK = 128
STRIP = 8


def split(value):
    high = value.astype(jnp.bfloat16)
    low = (value - high.astype(jnp.float32)).astype(jnp.bfloat16)
    return high, low


def dot_t(left, right):
    return lax.dot_general(
        left, right, (((0,), (0,)), ((), ())), preferred_element_type=jnp.float32
    )


def dot_3(left, right):
    left_high, left_low = split(left)
    right_high, right_low = split(right)
    dot = functools.partial(jnp.dot, preferred_element_type=jnp.float32)
    return dot(left_high, right_high) + dot(left_high, right_low) + dot(left_low, right_high)


def invert_factor(work):
    row = lax.broadcasted_iota(jnp.int32, (STRIP, 2 * BLOCK), 0)
    for strip in range(BLOCK // STRIP):
        start = strip * STRIP
        rows = work[start : start + STRIP, :]
        scale = jnp.zeros_like(rows)
        for step in range(STRIP):
            column = jnp.broadcast_to(
                rows[:, start + step : start + step + 1], (STRIP, 2 * BLOCK)
            )
            pivot = jnp.broadcast_to(column[step : step + 1, :], (STRIP, 2 * BLOCK))
            scale = jnp.where(row == step, pivot, scale)
            if step < STRIP - 1:
                pivot_row = jnp.broadcast_to(rows[step : step + 1, :], (STRIP, 2 * BLOCK))
                factor = jnp.where(row > step, column / pivot, 0.0)
                rows = rows - factor * pivot_row
        rows = rows * lax.rsqrt(scale)
        work[start : start + STRIP, :] = rows
        if start + STRIP < BLOCK:
            first = rows.astype(jnp.bfloat16).astype(jnp.float32)
            rest = rows - first
            second = rest.astype(jnp.bfloat16).astype(jnp.float32)
            third = rest - second
            right = jnp.concatenate([first, second, first, second, third, first], axis=0)
            left = jnp.concatenate([first, first, second, second, first, third], axis=0)
            update = dot_t(
                left[:, :BLOCK].astype(jnp.bfloat16), right.astype(jnp.bfloat16)
            )
            work[start + STRIP :, :] = work[start + STRIP :, :] - update[start + STRIP :, :]


def flip(index, mask_bits, log):
    total = 0
    for bit in range(log):
        place = 2**bit
        total = total + ((index // place + mask_bits // place) % 2) * place
    return total


def fused_kernel(
    axes, log, real, panel_ref, design_ref, weights_ref, out_ref,
    high_part, low_part, stage, panels, sums, landed, top, top_landed,
    done, work, block,
    stage_sem, panel_sem, panel_recv, panel_next, panel_pair,
    sum_send, sum_recv, top_send, top_recv, top_arrive, top_next, top_pair, out_sem,
):
    n_obs, n_unk = axes
    depth, _ = design_ref.shape
    chunks = panels.shape[0]
    width = chunks * BLOCK
    rows = high_part.shape[2]
    me = lax.axis_index("obs")
    unk = lax.axis_index("unk")
    odd = unk % 2
    even = odd == 0
    first = unk == 0
    has_next = jnp.logical_and(even, unk + 2 < n_unk)
    has_last = jnp.logical_and(even, unk >= 2)
    pair = unk + 1 - 2 * odd
    mesh_id = pl.DeviceIdType.MESH

    barrier = pltpu.get_barrier_semaphore()

    def greet(obs, other):
        pl.semaphore_signal(barrier, inc=1, device_id=(obs, other), device_id_type=mesh_id)

    for bit in range(log):
        greet(flip(me, 2**bit, log), unk)
    greet(me, pair)
    pl.when(has_next)(lambda: greet(me, unk + 2))
    pl.when(has_last)(lambda: greet(me, unk - 2))

    def load_panel(c):
        return pltpu.make_async_copy(
            panel_ref.at[:, pl.ds(pl.multiple_of(c * BLOCK, BLOCK), BLOCK)],
            panels.at[c], panel_sem.at[c],
        )

    def load_stage(piece, slot):
        size = stage.shape[1]
        return pltpu.make_async_copy(
            design_ref.at[pl.ds(pl.multiple_of(piece * size, size), size), :],
            stage.at[slot], stage_sem.at[slot],
        )

    @pl.when(first)
    def _():
        for c in range(chunks):
            load_panel(c).start()

    load_stage(0, 0).start()

    def remote(source, target, send, recv, obs, other):
        return pltpu.make_async_remote_copy(
            src_ref=source, dst_ref=target, send_sem=send, recv_sem=recv,
            device_id=(obs, other), device_id_type=mesh_id,
        )

    def panel_on(c):
        return remote(panels.at[c], panels.at[c], panel_next.at[c], panel_recv.at[c], me, unk + 2)

    def panel_across(c):
        return remote(panels.at[c], panels.at[c], panel_pair.at[c], panel_recv.at[c], me, pair)

    def top_on(c):
        return remote(top.at[c], top.at[c], top_next.at[c], top_arrive.at[c], me, unk + 2)

    def top_across(c):
        return remote(top.at[c], top.at[c], top_pair.at[c], top_arrive.at[c], me, pair)

    def forward_panel(c):
        pl.when(has_next)(lambda: panel_on(c).start())
        pl.when(even)(lambda: panel_across(c).start())

    chained = has_next.astype(jnp.int32) + has_last.astype(jnp.int32)
    pl.semaphore_wait(barrier, log + 1 + chained)

    @pl.when(first)
    def _():
        def send(c, _):
            load_panel(c).wait()
            forward_panel(c)
            return 0

        lax.fori_loop(0, chunks, send, 0)

    size = stage.shape[1]
    pieces = depth // size

    def split_piece(piece, _):
        slot = piece % 2
        pl.when(piece + 1 < pieces)(lambda: load_stage(piece + 1, 1 - slot).start())
        load_stage(piece, slot).wait()
        for owner in range(n_obs):
            high, low = split(stage[slot, :, owner * rows : (owner + 1) * rows])
            where = pl.ds(pl.multiple_of(piece * size, size), size)
            high_part[owner, where, :] = high
            low_part[owner, where, :] = low
        return 0

    lax.fori_loop(0, pieces, split_piece, 0)

    def turn(level):
        mask = (1 - odd) * 2**level + odd * 2 ** (log - 1 - level)
        spacing = (1 - odd) * 2 ** (level + 1) + odd
        return mask, spacing

    def place(level, item):
        return n_obs - 2 ** (log - level) + item

    def sum_copy(c, level, item):
        mask, spacing = turn(level)
        at = place(level, item)
        return remote(
            sums.at[c, item * spacing + mask], landed.at[c, at],
            sum_send.at[c, at], sum_recv.at[c, at], flip(me, mask, log), unk,
        )

    def top_copy(c, level):
        mask, _ = turn(level)
        return remote(
            top.at[c], top_landed.at[c, level],
            top_send.at[c, level], top_recv.at[c, level], flip(me, mask, log), unk,
        )

    def start_level(c, level):
        for item in range(2 ** (log - 1 - level)):
            sum_copy(c, level, item).start()
        pl.when(first)(lambda: top_copy(c, level).start())

    dot = functools.partial(jnp.dot, preferred_element_type=jnp.float32)

    def products(c):
        @pl.when(jnp.logical_not(first))
        def _():
            panel_across(c).wait_recv()
            forward_panel(c)

        weighted = jnp.transpose(panels[c] * weights_ref[...])
        high, low = split(weighted)
        both = jnp.concatenate([high, low], axis=0)

        def owner_block(q, _):
            owner = flip(me, q, log)
            wide = dot(both, high_part[owner])
            sums[c, q] = wide[:BLOCK] + wide[BLOCK:] + dot(high, low_part[owner])
            return 0

        lax.fori_loop(0, n_obs, owner_block, 0)

        @pl.when(first)
        def _():
            for owner in range(n_obs):
                start, stop = owner * real, min((owner + 1) * real, width)
                if start < stop:
                    top[c, :, start:stop] = sums[c, flip(me, owner, log), :, : stop - start]

        start_level(c, 0)

    def reduce_level(c, level):
        _, spacing = turn(level)
        for item in range(2 ** (log - 1 - level)):
            sum_copy(c, level, item).wait_recv()
            here = item * spacing
            sums[c, here] = sums[c, here] + landed[c, place(level, item)]

        @pl.when(first)
        def _():
            top_copy(c, level).wait()
            top[c] = top[c] + top_landed[c, level]

        if level + 1 < log:
            start_level(c, level + 1)
        else:
            @pl.when(first)
            def _():
                pl.when(has_next)(lambda: top_on(c).start())
                top_across(c).start()

    eye = (
        lax.broadcasted_iota(jnp.int32, (BLOCK, BLOCK), 0)
        == lax.broadcasted_iota(jnp.int32, (BLOCK, BLOCK), 1)
    ).astype(jnp.float32)

    def out_copy(c):
        return pltpu.make_async_copy(
            sums.at[c, 0],
            out_ref.at[pl.ds(pl.multiple_of(c * BLOCK, BLOCK), BLOCK), :],
            out_sem.at[c],
        )

    def factor(k):
        @pl.when(jnp.logical_not(first))
        def _():
            top_across(k).wait_recv()
            pl.when(has_next)(lambda: top_on(k).start())
            pl.when(even)(lambda: top_across(k).start())

        offset = pl.multiple_of(k * BLOCK, BLOCK)
        block[:, :width] = top[k]
        block[:, width:] = sums[k, 0]

        def earlier(j, _):
            held = done[j, :, pl.ds(offset, BLOCK)]
            swapped = jnp.concatenate([held[BLOCK:], held[:BLOCK]], axis=0)
            block[...] = block[...] - (
                dot_t(swapped, done[j]) + dot_t(held[:BLOCK], done[j, :BLOCK, :])
            )
            return 0

        lax.fori_loop(0, k, earlier, 0)
        work[:, :BLOCK] = block[:, pl.ds(offset, BLOCK)]
        work[:, BLOCK:] = eye
        invert_factor(work)
        column = dot_3(work[:, BLOCK:], block[...])
        high, low = split(column)
        done[k, :BLOCK, :] = high
        done[k, BLOCK:, :] = low
        sums[k, 0] = column[:, width:]
        out_copy(k).start()

    def step(t, _):
        pl.when(t < chunks)(lambda: products(t))
        for level in range(log):
            c = t - 1 - level
            pl.when(jnp.logical_and(c >= 0, c < chunks))(functools.partial(reduce_level, c, level))
        pl.when(t >= log + 1)(lambda: factor(t - log - 1))
        return 0

    lax.fori_loop(0, chunks + log + 1, step, 0)

    def drain(c, _):
        out_copy(c).wait()
        for level in range(log):
            for item in range(2 ** (log - 1 - level)):
                sum_copy(c, level, item).wait_send()

        @pl.when(has_next)
        def _():
            panel_on(c).wait_send()
            top_on(c).wait_send()

        @pl.when(even)
        def _():
            panel_across(c).wait_send()
            top_across(c).wait_send()

        return 0

    lax.fori_loop(0, chunks, drain, 0)


def fused(axes, real, panel, design, weights):
    n_obs, n_unk = axes
    log = n_obs.bit_length() - 1
    depth, columns = design.shape
    rows = columns // n_obs
    width = 2 * PANEL
    chunks = width // BLOCK
    piece = 64
    f32, bf16, dma = jnp.float32, jnp.bfloat16, pltpu.SemaphoreType.DMA
    return pl.pallas_call(
        functools.partial(fused_kernel, axes, log, real),
        out_shape=jax.ShapeDtypeStruct((width, rows), f32),
        in_specs=[
            pl.BlockSpec(memory_space=pl.ANY),
            pl.BlockSpec(memory_space=pl.ANY),
            pl.BlockSpec(memory_space=pltpu.VMEM),
        ],
        out_specs=pl.BlockSpec(memory_space=pl.ANY),
        scratch_shapes=[
            pltpu.VMEM((n_obs, depth, rows), bf16),
            pltpu.VMEM((n_obs, depth, rows), bf16),
            pltpu.VMEM((2, piece, columns), f32),
            pltpu.VMEM((chunks, depth, BLOCK), f32),
            pltpu.VMEM((chunks, n_obs, BLOCK, rows), f32),
            pltpu.VMEM((chunks, n_obs - 1, BLOCK, rows), f32),
            pltpu.VMEM((chunks, BLOCK, width), f32),
            pltpu.VMEM((chunks, log, BLOCK, width), f32),
            pltpu.VMEM((chunks, 2 * BLOCK, width + rows), bf16),
            pltpu.VMEM((BLOCK, 2 * BLOCK), f32),
            pltpu.VMEM((BLOCK, width + rows), f32),
            dma((2,)), dma((chunks,)), dma((chunks,)), dma((chunks,)), dma((chunks,)),
            dma((chunks, n_obs - 1)), dma((chunks, n_obs - 1)),
            dma((chunks, log)), dma((chunks, log)),
            dma((chunks,)), dma((chunks,)), dma((chunks,)), dma((chunks,)),
        ],
        compiler_params=pltpu.CompilerParams(
            collective_id=0, has_side_effects=True, vmem_limit_bytes=64 * 2**20 - 2**16
        ),
    )(panel, design, weights)


def local(axes, design, weights):
    n_obs, _ = axes
    depth, columns = design.shape
    rows = columns // n_obs
    padded = -(-rows // BLOCK) * BLOCK
    panel = design
    if padded != rows:
        design = jnp.pad(
            design.reshape(depth, n_obs, rows), ((0, 0), (0, 0), (0, padded - rows))
        ).reshape(depth, n_obs * padded)
    return fused(axes, rows, panel, design, weights[:, None])[:, :rows].T


def solution(mesh):
    axes = (mesh.shape["obs"], mesh.shape["unk"])
    return jax.shard_map(
        functools.partial(local, axes),
        mesh=mesh,
        in_specs=(P("obs", "unk"), P("obs")),
        out_specs=P(("unk", "obs"), None),
        check_vma=False,
    )
```

```python
import functools
import jax
import jax.numpy as jnp
from jax import lax
from jax.experimental import pallas as pl
from jax.experimental.pallas import tpu as pltpu
from jax.sharding import PartitionSpec as P

PANEL = 512
BLOCK = 128
STRIP = 16


def split(value):
    high = value.astype(jnp.bfloat16)
    low = (value - high.astype(jnp.float32)).astype(jnp.bfloat16)
    return high, low


def dot_t(left, right):
    return lax.dot_general(
        left, right, (((0,), (0,)), ((), ())), preferred_element_type=jnp.float32
    )


def dot_3(left, right):
    left_high, left_low = split(left)
    right_high, right_low = split(right)
    dot = functools.partial(jnp.dot, preferred_element_type=jnp.float32)
    return dot(left_high, right_high) + dot(left_high, right_low) + dot(left_low, right_high)


def spread_row(value, index):
    return jnp.broadcast_to(value[index : index + 1, :], value.shape)


def invert_factor(work):
    half = STRIP // 2
    row = lax.broadcasted_iota(jnp.int32, (half, BLOCK), 0)
    for strip in range(BLOCK // STRIP):
        start = strip * STRIP
        upper = work[start : start + half, :]
        lower = work[start + half : start + STRIP, :]

        def lanes(value, index):
            return jnp.broadcast_to(
                value[:, start + index : start + index + 1], (half, BLOCK)
            )

        columns_up = [lanes(upper, index) for index in range(STRIP)]
        columns_down = [lanes(lower, index) for index in range(STRIP)]
        rest_up = [upper[:, :BLOCK], upper[:, BLOCK:]]
        rest_down = [lower[:, :BLOCK], lower[:, BLOCK:]]
        scale_up = jnp.zeros((half, BLOCK), jnp.float32)
        scale_down = scale_up
        for step in range(half):
            pivot = spread_row(columns_up[step], step)
            scale_up = jnp.where(row == step, pivot, scale_up)
            inverse = 1.0 / pivot
            factor_up = jnp.where(row > step, columns_up[step] * inverse, 0.0)
            factor_down = columns_down[step] * inverse
            for up, down in ((columns_up, columns_down), (rest_up, rest_down)):
                for index in range(step + 1 if up is columns_up else 0, len(up)):
                    pivot_row = spread_row(up[index], step)
                    up[index] = up[index] - factor_up * pivot_row
                    down[index] = down[index] - factor_down * pivot_row
        for step in range(half):
            pivot = spread_row(columns_down[half + step], step)
            scale_down = jnp.where(row == step, pivot, scale_down)
            if step < half - 1:
                inverse = 1.0 / pivot
                factor_down = jnp.where(row > step, columns_down[half + step] * inverse, 0.0)
                for down, begin in ((columns_down, half + step + 1), (rest_down, 0)):
                    for index in range(begin, len(down)):
                        down[index] = down[index] - factor_down * spread_row(down[index], step)
        root_up, root_down = lax.rsqrt(scale_up), lax.rsqrt(scale_down)
        rows = jnp.concatenate(
            [
                jnp.concatenate([value * root_up for value in rest_up], axis=1),
                jnp.concatenate([value * root_down for value in rest_down], axis=1),
            ],
            axis=0,
        )
        work[start : start + STRIP, :] = rows
        if start + STRIP < BLOCK:
            first = rows.astype(jnp.bfloat16)
            rest = rows - first.astype(jnp.float32)
            second = rest.astype(jnp.bfloat16)
            third = (rest - second.astype(jnp.float32)).astype(jnp.bfloat16)
            right = jnp.concatenate([first, second, first, second, third, first], axis=0)
            left = jnp.concatenate([first, first, second, second, first, third], axis=0)
            update = dot_t(left[:, :BLOCK], right)
            work[start + STRIP :, :] = work[start + STRIP :, :] - update[start + STRIP :, :]


def flip(index, mask_bits, log):
    total = 0
    for bit in range(log):
        place = 2**bit
        total = total + ((index // place + mask_bits // place) % 2) * place
    return total


def fused_kernel(
    axes, log, real, panel_ref, design_ref, weights_ref, out_ref,
    high_part, low_part, stage, panels, sums, landed, top, top_landed,
    done, work, block,
    stage_sem, panel_sem, panel_recv, panel_next, panel_pair,
    sum_send, sum_recv, top_send, top_recv, top_arrive, top_next, top_pair, out_sem,
):
    n_obs, n_unk = axes
    depth, _ = design_ref.shape
    chunks = panels.shape[0]
    width = chunks * BLOCK
    rows = high_part.shape[2]
    me = lax.axis_index("obs")
    unk = lax.axis_index("unk")
    odd = unk % 2
    even = odd == 0
    first = unk == 0
    has_next = jnp.logical_and(even, unk + 2 < n_unk)
    has_last = jnp.logical_and(even, unk >= 2)
    pair = unk + 1 - 2 * odd
    mesh_id = pl.DeviceIdType.MESH

    barrier = pltpu.get_barrier_semaphore()

    def greet(obs, other):
        pl.semaphore_signal(barrier, inc=1, device_id=(obs, other), device_id_type=mesh_id)

    for bit in range(log):
        greet(flip(me, 2**bit, log), unk)
    greet(me, pair)
    pl.when(has_next)(lambda: greet(me, unk + 2))
    pl.when(has_last)(lambda: greet(me, unk - 2))

    def load_panel(c):
        return pltpu.make_async_copy(
            panel_ref.at[:, pl.ds(pl.multiple_of(c * BLOCK, BLOCK), BLOCK)],
            panels.at[c], panel_sem.at[c],
        )

    def load_stage(piece, slot):
        size = stage.shape[1]
        return pltpu.make_async_copy(
            design_ref.at[pl.ds(pl.multiple_of(piece * size, size), size), :],
            stage.at[slot], stage_sem.at[slot],
        )

    @pl.when(first)
    def _():
        for c in range(chunks):
            load_panel(c).start()

    load_stage(0, 0).start()

    def remote(source, target, send, recv, obs, other):
        return pltpu.make_async_remote_copy(
            src_ref=source, dst_ref=target, send_sem=send, recv_sem=recv,
            device_id=(obs, other), device_id_type=mesh_id,
        )

    def panel_on(c):
        return remote(panels.at[c], panels.at[c], panel_next.at[c], panel_recv.at[c], me, unk + 2)

    def panel_across(c):
        return remote(panels.at[c], panels.at[c], panel_pair.at[c], panel_recv.at[c], me, pair)

    def top_on(c):
        return remote(top.at[c], top.at[c], top_next.at[c], top_arrive.at[c], me, unk + 2)

    def top_across(c):
        return remote(top.at[c], top.at[c], top_pair.at[c], top_arrive.at[c], me, pair)

    def forward_panel(c):
        pl.when(has_next)(lambda: panel_on(c).start())
        pl.when(even)(lambda: panel_across(c).start())

    chained = has_next.astype(jnp.int32) + has_last.astype(jnp.int32)
    pl.semaphore_wait(barrier, log + 1 + chained)

    @pl.when(first)
    def _():
        def send(c, _):
            load_panel(c).wait()
            forward_panel(c)
            return 0

        lax.fori_loop(0, chunks, send, 0)

    size = stage.shape[1]
    pieces = depth // size

    def split_piece(piece, _):
        slot = piece % 2
        pl.when(piece + 1 < pieces)(lambda: load_stage(piece + 1, 1 - slot).start())
        load_stage(piece, slot).wait()
        for owner in range(n_obs):
            high, low = split(stage[slot, :, owner * rows : (owner + 1) * rows])
            where = pl.ds(pl.multiple_of(piece * size, size), size)
            high_part[owner, where, :] = high
            low_part[owner, where, :] = low
        return 0

    lax.fori_loop(0, pieces, split_piece, 0)

    def turn(level):
        mask = (1 - odd) * 2**level + odd * 2 ** (log - 1 - level)
        spacing = (1 - odd) * 2 ** (level + 1) + odd
        return mask, spacing

    def place(level, item):
        return n_obs - 2 ** (log - level) + item

    def sum_copy(c, level, item):
        mask, spacing = turn(level)
        at = place(level, item)
        return remote(
            sums.at[c, item * spacing + mask], landed.at[c, at],
            sum_send.at[c, at], sum_recv.at[c, at], flip(me, mask, log), unk,
        )

    def top_copy(c, level):
        mask, _ = turn(level)
        return remote(
            top.at[c], top_landed.at[c, level],
            top_send.at[c, level], top_recv.at[c, level], flip(me, mask, log), unk,
        )

    def start_level(c, level):
        for item in range(2 ** (log - 1 - level)):
            sum_copy(c, level, item).start()
        pl.when(first)(lambda: top_copy(c, level).start())

    dot = functools.partial(jnp.dot, preferred_element_type=jnp.float32)

    def products(c):
        @pl.when(jnp.logical_not(first))
        def _():
            panel_across(c).wait_recv()
            forward_panel(c)

        weighted = jnp.transpose(panels[c] * weights_ref[...])
        high, low = split(weighted)
        both = jnp.concatenate([high, low], axis=0)

        def owner_block(q, _):
            owner = flip(me, q, log)
            wide = dot(both, high_part[owner])
            sums[c, q] = wide[:BLOCK] + wide[BLOCK:] + dot(high, low_part[owner])
            return 0

        lax.fori_loop(0, n_obs, owner_block, 0)

        @pl.when(first)
        def _():
            for owner in range(n_obs):
                start, stop = owner * real, min((owner + 1) * real, width)
                if start < stop:
                    top[c, :, start:stop] = sums[c, flip(me, owner, log), :, : stop - start]

        start_level(c, 0)

    def reduce_level(c, level):
        _, spacing = turn(level)
        for item in range(2 ** (log - 1 - level)):
            sum_copy(c, level, item).wait_recv()
            here = item * spacing
            sums[c, here] = sums[c, here] + landed[c, place(level, item)]

        @pl.when(first)
        def _():
            top_copy(c, level).wait()
            top[c] = top[c] + top_landed[c, level]

        if level + 1 < log:
            start_level(c, level + 1)
        else:
            @pl.when(first)
            def _():
                pl.when(has_next)(lambda: top_on(c).start())
                top_across(c).start()

    eye = (
        lax.broadcasted_iota(jnp.int32, (BLOCK, BLOCK), 0)
        == lax.broadcasted_iota(jnp.int32, (BLOCK, BLOCK), 1)
    ).astype(jnp.float32)

    def out_copy(c):
        return pltpu.make_async_copy(
            sums.at[c, 0],
            out_ref.at[pl.ds(pl.multiple_of(c * BLOCK, BLOCK), BLOCK), :],
            out_sem.at[c],
        )

    def factor(k):
        @pl.when(jnp.logical_not(first))
        def _():
            top_across(k).wait_recv()
            pl.when(has_next)(lambda: top_on(k).start())
            pl.when(even)(lambda: top_across(k).start())

        offset = pl.multiple_of(k * BLOCK, BLOCK)
        block[:, :width] = top[k]
        block[:, width:] = sums[k, 0]

        def earlier(j, _):
            held = done[j, :, pl.ds(offset, BLOCK)]
            swapped = jnp.concatenate([held[BLOCK:], held[:BLOCK]], axis=0)
            block[...] = block[...] - (
                dot_t(swapped, done[j]) + dot_t(held[:BLOCK], done[j, :BLOCK, :])
            )
            return 0

        lax.fori_loop(0, k, earlier, 0)
        work[:, :BLOCK] = block[:, pl.ds(offset, BLOCK)]
        work[:, BLOCK:] = eye
        invert_factor(work)
        column = dot_3(work[:, BLOCK:], block[...])
        high, low = split(column)
        done[k, :BLOCK, :] = high
        done[k, BLOCK:, :] = low
        sums[k, 0] = column[:, width:]
        out_copy(k).start()

    def step(t, _):
        pl.when(t < chunks)(lambda: products(t))
        for level in range(log):
            c = t - 1 - level
            pl.when(jnp.logical_and(c >= 0, c < chunks))(functools.partial(reduce_level, c, level))
        pl.when(t >= log + 1)(lambda: factor(t - log - 1))
        return 0

    lax.fori_loop(0, chunks + log + 1, step, 0)

    def drain(c, _):
        out_copy(c).wait()
        for level in range(log):
            for item in range(2 ** (log - 1 - level)):
                sum_copy(c, level, item).wait_send()

        @pl.when(has_next)
        def _():
            panel_on(c).wait_send()
            top_on(c).wait_send()

        @pl.when(even)
        def _():
            panel_across(c).wait_send()
            top_across(c).wait_send()

        return 0

    lax.fori_loop(0, chunks, drain, 0)


def fused(axes, real, panel, design, weights):
    n_obs, n_unk = axes
    log = n_obs.bit_length() - 1
    depth, columns = design.shape
    rows = columns // n_obs
    width = 2 * PANEL
    chunks = width // BLOCK
    piece = 64
    f32, bf16, dma = jnp.float32, jnp.bfloat16, pltpu.SemaphoreType.DMA
    return pl.pallas_call(
        functools.partial(fused_kernel, axes, log, real),
        out_shape=jax.ShapeDtypeStruct((width, rows), f32),
        in_specs=[
            pl.BlockSpec(memory_space=pl.ANY),
            pl.BlockSpec(memory_space=pl.ANY),
            pl.BlockSpec(memory_space=pltpu.VMEM),
        ],
        out_specs=pl.BlockSpec(memory_space=pl.ANY),
        scratch_shapes=[
            pltpu.VMEM((n_obs, depth, rows), bf16),
            pltpu.VMEM((n_obs, depth, rows), bf16),
            pltpu.VMEM((2, piece, columns), f32),
            pltpu.VMEM((chunks, depth, BLOCK), f32),
            pltpu.VMEM((chunks, n_obs, BLOCK, rows), f32),
            pltpu.VMEM((chunks, n_obs - 1, BLOCK, rows), f32),
            pltpu.VMEM((chunks, BLOCK, width), f32),
            pltpu.VMEM((chunks, log, BLOCK, width), f32),
            pltpu.VMEM((chunks, 2 * BLOCK, width + rows), bf16),
            pltpu.VMEM((BLOCK, 2 * BLOCK), f32),
            pltpu.VMEM((BLOCK, width + rows), f32),
            dma((2,)), dma((chunks,)), dma((chunks,)), dma((chunks,)), dma((chunks,)),
            dma((chunks, n_obs - 1)), dma((chunks, n_obs - 1)),
            dma((chunks, log)), dma((chunks, log)),
            dma((chunks,)), dma((chunks,)), dma((chunks,)), dma((chunks,)),
        ],
        compiler_params=pltpu.CompilerParams(
            collective_id=0, has_side_effects=True, vmem_limit_bytes=64 * 2**20 - 2**16
        ),
    )(panel, design, weights)


def local(axes, design, weights):
    n_obs, _ = axes
    depth, columns = design.shape
    rows = columns // n_obs
    padded = -(-rows // BLOCK) * BLOCK
    panel = design
    if padded != rows:
        design = jnp.pad(
            design.reshape(depth, n_obs, rows), ((0, 0), (0, 0), (0, padded - rows))
        ).reshape(depth, n_obs * padded)
    return fused(axes, rows, panel, design, weights[:, None])[:, :rows].T


def solution(mesh):
    axes = (mesh.shape["obs"], mesh.shape["unk"])
    return jax.shard_map(
        functools.partial(local, axes),
        mesh=mesh,
        in_specs=(P("obs", "unk"), P("obs")),
        out_specs=P(("unk", "obs"), None),
        check_vma=False,
    )
```

```python
import functools
import jax
import jax.numpy as jnp
from jax import lax
from jax.experimental import pallas as pl
from jax.experimental.pallas import tpu as pltpu
from jax.sharding import PartitionSpec as P

PANEL = 512
BLOCK = 128
STRIP = 16
GROUP = 2


def split(value):
    high = value.astype(jnp.bfloat16)
    low = (value - high.astype(jnp.float32)).astype(jnp.bfloat16)
    return high, low


def dot_t(left, right):
    return lax.dot_general(
        left, right, (((0,), (0,)), ((), ())), preferred_element_type=jnp.float32
    )


def dot_3(left, right):
    left_high, left_low = split(left)
    right_high, right_low = split(right)
    dot = functools.partial(jnp.dot, preferred_element_type=jnp.float32)
    return dot(left_high, right_high) + dot(left_high, right_low) + dot(left_low, right_high)


def spread_row(value, index):
    return jnp.broadcast_to(value[index : index + 1, :], value.shape)


def invert_factor(work):
    half = STRIP // 2
    row = lax.broadcasted_iota(jnp.int32, (half, BLOCK), 0)
    for strip in range(BLOCK // STRIP):
        start = strip * STRIP
        upper = work[start : start + half, :]
        lower = work[start + half : start + STRIP, :]

        def lanes(value, index):
            return jnp.broadcast_to(
                value[:, start + index : start + index + 1], (half, BLOCK)
            )

        columns_up = [lanes(upper, index) for index in range(STRIP)]
        columns_down = [lanes(lower, index) for index in range(STRIP)]
        rest_up = [upper[:, :BLOCK], upper[:, BLOCK:]]
        rest_down = [lower[:, :BLOCK], lower[:, BLOCK:]]
        scale_up = jnp.zeros((half, BLOCK), jnp.float32)
        scale_down = scale_up
        for step in range(half):
            pivot = spread_row(columns_up[step], step)
            scale_up = jnp.where(row == step, pivot, scale_up)
            inverse = 1.0 / pivot
            factor_up = jnp.where(row > step, columns_up[step] * inverse, 0.0)
            factor_down = columns_down[step] * inverse
            for up, down in ((columns_up, columns_down), (rest_up, rest_down)):
                for index in range(step + 1 if up is columns_up else 0, len(up)):
                    pivot_row = spread_row(up[index], step)
                    up[index] = up[index] - factor_up * pivot_row
                    down[index] = down[index] - factor_down * pivot_row
        for step in range(half):
            pivot = spread_row(columns_down[half + step], step)
            scale_down = jnp.where(row == step, pivot, scale_down)
            if step < half - 1:
                inverse = 1.0 / pivot
                factor_down = jnp.where(row > step, columns_down[half + step] * inverse, 0.0)
                for down, begin in ((columns_down, half + step + 1), (rest_down, 0)):
                    for index in range(begin, len(down)):
                        down[index] = down[index] - factor_down * spread_row(down[index], step)
        root_up, root_down = lax.rsqrt(scale_up), lax.rsqrt(scale_down)
        rows = jnp.concatenate(
            [
                jnp.concatenate([value * root_up for value in rest_up], axis=1),
                jnp.concatenate([value * root_down for value in rest_down], axis=1),
            ],
            axis=0,
        )
        work[start : start + STRIP, :] = rows
        if start + STRIP < BLOCK:
            first = rows.astype(jnp.bfloat16)
            rest = rows - first.astype(jnp.float32)
            second = rest.astype(jnp.bfloat16)
            third = (rest - second.astype(jnp.float32)).astype(jnp.bfloat16)
            right = jnp.concatenate([first, second, first, second, third, first], axis=0)
            left = jnp.concatenate([first, first, second, second, first, third], axis=0)
            update = dot_t(left[:, :BLOCK], right)
            work[start + STRIP :, :] = work[start + STRIP :, :] - update[start + STRIP :, :]


def flip(index, mask_bits, log):
    total = 0
    for bit in range(log):
        place = 2**bit
        total = total + ((index // place + mask_bits // place) % 2) * place
    return total


def fused_kernel(
    axes, log, real, panel_ref, design_ref, weights_ref, out_ref,
    high_part, low_part, stage, panels, sums, landed, top, top_landed,
    done, work, block,
    stage_sem, panel_sem, panel_recv, panel_next, panel_pair,
    sum_send, sum_recv, top_send, top_recv, top_arrive, top_next, top_pair, out_sem,
):
    n_obs, n_unk = axes
    depth, _ = design_ref.shape
    chunks = panels.shape[0]
    width = chunks * BLOCK
    rows = high_part.shape[2]
    me = lax.axis_index("obs")
    unk = lax.axis_index("unk")
    odd = unk % 2
    even = odd == 0
    first = unk == 0
    has_next = jnp.logical_and(even, unk + 2 < n_unk)
    has_last = jnp.logical_and(even, unk >= 2)
    pair = unk + 1 - 2 * odd
    mesh_id = pl.DeviceIdType.MESH

    barrier = pltpu.get_barrier_semaphore()

    def greet(obs, other):
        pl.semaphore_signal(barrier, inc=1, device_id=(obs, other), device_id_type=mesh_id)

    for bit in range(log):
        greet(flip(me, 2**bit, log), unk)
    greet(me, pair)
    pl.when(has_next)(lambda: greet(me, unk + 2))
    pl.when(has_last)(lambda: greet(me, unk - 2))

    def load_panel(c):
        return pltpu.make_async_copy(
            panel_ref.at[:, pl.ds(pl.multiple_of(c * BLOCK, BLOCK), BLOCK)],
            panels.at[c], panel_sem.at[c],
        )

    def load_stage(piece, slot):
        size = stage.shape[1]
        return pltpu.make_async_copy(
            design_ref.at[pl.ds(pl.multiple_of(piece * size, size), size), :],
            stage.at[slot], stage_sem.at[slot],
        )

    @pl.when(first)
    def _():
        for c in range(chunks):
            load_panel(c).start()

    load_stage(0, 0).start()

    def remote(source, target, send, recv, obs, other):
        return pltpu.make_async_remote_copy(
            src_ref=source, dst_ref=target, send_sem=send, recv_sem=recv,
            device_id=(obs, other), device_id_type=mesh_id,
        )

    def panel_on(c):
        return remote(panels.at[c], panels.at[c], panel_next.at[c], panel_recv.at[c], me, unk + 2)

    def panel_across(c):
        return remote(panels.at[c], panels.at[c], panel_pair.at[c], panel_recv.at[c], me, pair)

    def in_group(c, action):
        for group in range(chunks // GROUP):
            pl.when(c // GROUP == group)(functools.partial(action, group * GROUP * BLOCK))

    def top_on(c, begin):
        part = top.at[c, :, begin:]
        return remote(part, part, top_next.at[c], top_arrive.at[c], me, unk + 2)

    def top_across(c, begin):
        part = top.at[c, :, begin:]
        return remote(part, part, top_pair.at[c], top_arrive.at[c], me, pair)

    def forward_top(c, begin):
        pl.when(has_next)(lambda: top_on(c, begin).start())
        pl.when(even)(lambda: top_across(c, begin).start())

    def forward_panel(c):
        pl.when(has_next)(lambda: panel_on(c).start())
        pl.when(even)(lambda: panel_across(c).start())

    chained = has_next.astype(jnp.int32) + has_last.astype(jnp.int32)
    pl.semaphore_wait(barrier, log + 1 + chained)

    @pl.when(first)
    def _():
        def send(c, _):
            load_panel(c).wait()
            forward_panel(c)
            return 0

        lax.fori_loop(0, chunks, send, 0)

    size = stage.shape[1]
    pieces = depth // size

    def split_piece(piece, _):
        slot = piece % 2
        pl.when(piece + 1 < pieces)(lambda: load_stage(piece + 1, 1 - slot).start())
        load_stage(piece, slot).wait()
        for owner in range(n_obs):
            high, low = split(stage[slot, :, owner * rows : (owner + 1) * rows])
            where = pl.ds(pl.multiple_of(piece * size, size), size)
            high_part[owner, where, :] = high
            low_part[owner, where, :] = low
        return 0

    lax.fori_loop(0, pieces, split_piece, 0)

    def turn(level):
        mask = (1 - odd) * 2**level + odd * 2 ** (log - 1 - level)
        spacing = (1 - odd) * 2 ** (level + 1) + odd
        return mask, spacing

    def place(level, item):
        return n_obs - 2 ** (log - level) + item

    def sum_copy(c, level, item):
        mask, spacing = turn(level)
        at = place(level, item)
        return remote(
            sums.at[c, item * spacing + mask], landed.at[c, at],
            sum_send.at[c, at], sum_recv.at[c, at], flip(me, mask, log), unk,
        )

    def top_copy(c, level, begin):
        mask, _ = turn(level)
        return remote(
            top.at[c, :, begin:], top_landed.at[c, level, :, begin:],
            top_send.at[c, level], top_recv.at[c, level], flip(me, mask, log), unk,
        )

    def start_level(c, level):
        for item in range(2 ** (log - 1 - level)):
            sum_copy(c, level, item).start()
        pl.when(first)(lambda: in_group(c, lambda begin: top_copy(c, level, begin).start()))

    dot = functools.partial(jnp.dot, preferred_element_type=jnp.float32)

    def products(c):
        @pl.when(jnp.logical_not(first))
        def _():
            panel_across(c).wait_recv()
            forward_panel(c)

        weighted = jnp.transpose(panels[c]) * weights_ref[...]
        high, low = split(weighted)
        both = jnp.concatenate([high, low], axis=0)

        def owner_block(q, _):
            owner = flip(me, q, log)
            wide = dot(both, high_part[owner])
            sums[c, q] = wide[:BLOCK] + wide[BLOCK:] + dot(high, low_part[owner])
            return 0

        lax.fori_loop(0, n_obs, owner_block, 0)

        @pl.when(first)
        def _():
            for owner in range(n_obs):
                start, stop = owner * real, min((owner + 1) * real, width)
                if start < stop:
                    top[c, :, start:stop] = sums[c, flip(me, owner, log), :, : stop - start]

        start_level(c, 0)

    def reduce_level(c, level):
        _, spacing = turn(level)
        for item in range(2 ** (log - 1 - level)):
            sum_copy(c, level, item).wait_recv()
            here = item * spacing
            sums[c, here] = sums[c, here] + landed[c, place(level, item)]

        @pl.when(first)
        def _():
            def add(begin):
                top_copy(c, level, begin).wait()
                top[c, :, begin:] = top[c, :, begin:] + top_landed[c, level, :, begin:]

            in_group(c, add)

        if level + 1 < log:
            start_level(c, level + 1)
        else:
            pl.when(first)(lambda: in_group(c, functools.partial(forward_top, c)))

    eye = (
        lax.broadcasted_iota(jnp.int32, (BLOCK, BLOCK), 0)
        == lax.broadcasted_iota(jnp.int32, (BLOCK, BLOCK), 1)
    ).astype(jnp.float32)

    def out_copy(c):
        return pltpu.make_async_copy(
            sums.at[c, 0],
            out_ref.at[pl.ds(pl.multiple_of(c * BLOCK, BLOCK), BLOCK), :],
            out_sem.at[c],
        )

    def factor(k):
        @pl.when(jnp.logical_not(first))
        def _():
            def arrive(begin):
                top_across(k, begin).wait_recv()
                forward_top(k, begin)

            in_group(k, arrive)

        offset = pl.multiple_of(k * BLOCK, BLOCK)

        def update(begin):
            block[:, begin:width] = top[k, :, begin:]
            block[:, width:] = sums[k, 0]

            def earlier(j, _):
                held = done[j, :, pl.ds(offset, BLOCK)]
                swapped = jnp.concatenate([held[BLOCK:], held[:BLOCK]], axis=0)
                block[:, begin:] = block[:, begin:] - (
                    dot_t(swapped, done[j, :, begin:])
                    + dot_t(held[:BLOCK], done[j, :BLOCK, begin:])
                )
                return 0

            lax.fori_loop(0, k, earlier, 0)

        in_group(k, update)
        work[:, :BLOCK] = block[:, pl.ds(offset, BLOCK)]
        work[:, BLOCK:] = eye
        invert_factor(work)

        def solve(begin):
            column = dot_3(work[:, BLOCK:], block[:, begin:])
            high, low = split(column)
            done[k, :BLOCK, begin:] = high
            done[k, BLOCK:, begin:] = low
            sums[k, 0] = column[:, width - begin :]

        in_group(k, solve)
        out_copy(k).start()

    def step(t, _):
        pl.when(t < chunks)(lambda: products(t))
        for level in range(log):
            c = t - 1 - level
            pl.when(jnp.logical_and(c >= 0, c < chunks))(functools.partial(reduce_level, c, level))
        pl.when(t >= log)(lambda: factor(t - log))
        return 0

    lax.fori_loop(0, chunks + log, step, 0)

    def drain(c, _):
        out_copy(c).wait()
        for level in range(log):
            for item in range(2 ** (log - 1 - level)):
                sum_copy(c, level, item).wait_send()

        @pl.when(has_next)
        def _():
            panel_on(c).wait_send()
            in_group(c, lambda begin: top_on(c, begin).wait_send())

        @pl.when(even)
        def _():
            panel_across(c).wait_send()
            in_group(c, lambda begin: top_across(c, begin).wait_send())

        return 0

    lax.fori_loop(0, chunks, drain, 0)


def fused(axes, real, panel, design, weights):
    n_obs, n_unk = axes
    log = n_obs.bit_length() - 1
    depth, columns = design.shape
    rows = columns // n_obs
    width = 2 * PANEL
    chunks = width // BLOCK
    piece = 64
    f32, bf16, dma = jnp.float32, jnp.bfloat16, pltpu.SemaphoreType.DMA
    return pl.pallas_call(
        functools.partial(fused_kernel, axes, log, real),
        out_shape=jax.ShapeDtypeStruct((width, rows), f32),
        in_specs=[
            pl.BlockSpec(memory_space=pl.ANY),
            pl.BlockSpec(memory_space=pl.ANY),
            pl.BlockSpec(memory_space=pltpu.VMEM),
        ],
        out_specs=pl.BlockSpec(memory_space=pl.ANY),
        scratch_shapes=[
            pltpu.VMEM((n_obs, depth, rows), bf16),
            pltpu.VMEM((n_obs, depth, rows), bf16),
            pltpu.VMEM((2, piece, columns), f32),
            pltpu.VMEM((chunks, depth, BLOCK), f32),
            pltpu.VMEM((chunks, n_obs, BLOCK, rows), f32),
            pltpu.VMEM((chunks, n_obs - 1, BLOCK, rows), f32),
            pltpu.VMEM((chunks, BLOCK, width), f32),
            pltpu.VMEM((chunks, log, BLOCK, width), f32),
            pltpu.VMEM((chunks, 2 * BLOCK, width + rows), bf16),
            pltpu.VMEM((BLOCK, 2 * BLOCK), f32),
            pltpu.VMEM((BLOCK, width + rows), f32),
            dma((2,)), dma((chunks,)), dma((chunks,)), dma((chunks,)), dma((chunks,)),
            dma((chunks, n_obs - 1)), dma((chunks, n_obs - 1)),
            dma((chunks, log)), dma((chunks, log)),
            dma((chunks,)), dma((chunks,)), dma((chunks,)), dma((chunks,)),
        ],
        compiler_params=pltpu.CompilerParams(
            collective_id=0, has_side_effects=True, vmem_limit_bytes=64 * 2**20 - 2**16
        ),
    )(panel, design, weights)


def local(axes, design, weights):
    n_obs, _ = axes
    depth, columns = design.shape
    rows = columns // n_obs
    padded = -(-rows // BLOCK) * BLOCK
    panel = design
    if padded != rows:
        design = jnp.pad(
            design.reshape(depth, n_obs, rows), ((0, 0), (0, 0), (0, padded - rows))
        ).reshape(depth, n_obs * padded)
    return fused(axes, rows, panel, design, weights[None, :])[:, :rows].T


def solution(mesh):
    axes = (mesh.shape["obs"], mesh.shape["unk"])
    return jax.shard_map(
        functools.partial(local, axes),
        mesh=mesh,
        in_specs=(P("obs", "unk"), P("obs")),
        out_specs=P(("unk", "obs"), None),
        check_vma=False,
    )
```

```python
import functools
import jax
import jax.numpy as jnp
from jax import lax
from jax.experimental import pallas as pl
from jax.experimental.pallas import tpu as pltpu
from jax.sharding import PartitionSpec as P

PANEL = 512
BLOCK = 128
STRIP = 16
GROUP = 2
PARTS = 4


def split(value):
    high = value.astype(jnp.bfloat16)
    low = (value - high.astype(jnp.float32)).astype(jnp.bfloat16)
    return high, low


def dot_t(left, right):
    return lax.dot_general(
        left, right, (((0,), (0,)), ((), ())), preferred_element_type=jnp.float32
    )


def dot_3(left, right):
    left_high, left_low = split(left)
    right_high, right_low = split(right)
    dot = functools.partial(jnp.dot, preferred_element_type=jnp.float32)
    return dot(left_high, right_high) + dot(left_high, right_low) + dot(left_low, right_high)


def spread_row(value, index):
    return jnp.broadcast_to(value[index : index + 1, :], value.shape)


def invert_factor(work):
    half = STRIP // 2
    row = lax.broadcasted_iota(jnp.int32, (half, BLOCK), 0)
    for strip in range(BLOCK // STRIP):
        start = strip * STRIP
        upper = work[start : start + half, :]
        lower = work[start + half : start + STRIP, :]

        def lanes(value, index):
            return jnp.broadcast_to(
                value[:, start + index : start + index + 1], (half, BLOCK)
            )

        columns_up = [lanes(upper, index) for index in range(STRIP)]
        columns_down = [lanes(lower, index) for index in range(STRIP)]
        rest_up = [upper[:, :BLOCK], upper[:, BLOCK:]]
        rest_down = [lower[:, :BLOCK], lower[:, BLOCK:]]
        scale_up = jnp.zeros((half, BLOCK), jnp.float32)
        scale_down = scale_up
        for step in range(half):
            pivot = spread_row(columns_up[step], step)
            scale_up = jnp.where(row == step, pivot, scale_up)
            inverse = 1.0 / pivot
            factor_up = jnp.where(row > step, columns_up[step] * inverse, 0.0)
            factor_down = columns_down[step] * inverse
            for up, down in ((columns_up, columns_down), (rest_up, rest_down)):
                for index in range(step + 1 if up is columns_up else 0, len(up)):
                    pivot_row = spread_row(up[index], step)
                    up[index] = up[index] - factor_up * pivot_row
                    down[index] = down[index] - factor_down * pivot_row
        for step in range(half):
            pivot = spread_row(columns_down[half + step], step)
            scale_down = jnp.where(row == step, pivot, scale_down)
            if step < half - 1:
                inverse = 1.0 / pivot
                factor_down = jnp.where(row > step, columns_down[half + step] * inverse, 0.0)
                for down, begin in ((columns_down, half + step + 1), (rest_down, 0)):
                    for index in range(begin, len(down)):
                        down[index] = down[index] - factor_down * spread_row(down[index], step)
        root_up, root_down = lax.rsqrt(scale_up), lax.rsqrt(scale_down)
        rows = jnp.concatenate(
            [
                jnp.concatenate([value * root_up for value in rest_up], axis=1),
                jnp.concatenate([value * root_down for value in rest_down], axis=1),
            ],
            axis=0,
        )
        work[start : start + STRIP, :] = rows
        if start + STRIP < BLOCK:
            first = rows.astype(jnp.bfloat16)
            rest = rows - first.astype(jnp.float32)
            second = rest.astype(jnp.bfloat16)
            third = (rest - second.astype(jnp.float32)).astype(jnp.bfloat16)
            right = jnp.concatenate([first, second, first, second, third, first], axis=0)
            left = jnp.concatenate([first, first, second, second, first, third], axis=0)
            update = dot_t(left[:, :BLOCK], right)
            work[start + STRIP :, :] = work[start + STRIP :, :] - update[start + STRIP :, :]


def flip(index, mask_bits, log):
    total = 0
    for bit in range(log):
        place = 2**bit
        total = total + ((index // place + mask_bits // place) % 2) * place
    return total


def fused_kernel(
    axes, log, real, panel_ref, design_ref, weights_ref, out_ref,
    high_part, low_part, stage, panels, sums, landed, top, top_landed,
    done, work, block,
    stage_sem, panel_sem, panel_recv, panel_next, panel_pair,
    sum_send, sum_recv, top_send, top_recv, top_arrive, top_next, top_pair, out_sem,
):
    n_obs, n_unk = axes
    depth, _ = design_ref.shape
    chunks = panels.shape[0]
    width = chunks * BLOCK
    rows = high_part.shape[2]
    me = lax.axis_index("obs")
    unk = lax.axis_index("unk")
    odd = unk % 2
    even = odd == 0
    first = unk == 0
    has_next = jnp.logical_and(even, unk + 2 < n_unk)
    has_last = jnp.logical_and(even, unk >= 2)
    pair = unk + 1 - 2 * odd
    mesh_id = pl.DeviceIdType.MESH

    barrier = pltpu.get_barrier_semaphore()

    def greet(obs, other):
        pl.semaphore_signal(barrier, inc=1, device_id=(obs, other), device_id_type=mesh_id)

    for bit in range(log):
        greet(flip(me, 2**bit, log), unk)
    greet(me, pair)
    pl.when(has_next)(lambda: greet(me, unk + 2))
    pl.when(has_last)(lambda: greet(me, unk - 2))

    def load_panel(c):
        return pltpu.make_async_copy(
            panel_ref.at[:, pl.ds(pl.multiple_of(c * BLOCK, BLOCK), BLOCK)],
            panels.at[c], panel_sem.at[c],
        )

    def load_stage(piece, slot):
        size = stage.shape[1]
        return pltpu.make_async_copy(
            design_ref.at[pl.ds(pl.multiple_of(piece * size, size), size), :],
            stage.at[slot], stage_sem.at[slot],
        )

    @pl.when(first)
    def _():
        for c in range(chunks):
            load_panel(c).start()

    load_stage(0, 0).start()

    def remote(source, target, send, recv, obs, other):
        return pltpu.make_async_remote_copy(
            src_ref=source, dst_ref=target, send_sem=send, recv_sem=recv,
            device_id=(obs, other), device_id_type=mesh_id,
        )

    part_rows = depth // PARTS

    def panel_on(c, h):
        part = panels.at[c, h * part_rows : (h + 1) * part_rows, :]
        return remote(part, part, panel_next.at[c, h], panel_recv.at[c, h], me, unk + 2)

    def panel_across(c, h):
        part = panels.at[c, h * part_rows : (h + 1) * part_rows, :]
        return remote(part, part, panel_pair.at[c, h], panel_recv.at[c, h], me, pair)

    def in_group(c, action):
        for group in range(chunks // GROUP):
            pl.when(c // GROUP == group)(functools.partial(action, group * GROUP * BLOCK))

    def top_on(c, begin):
        part = top.at[c, :, begin:]
        return remote(part, part, top_next.at[c], top_arrive.at[c], me, unk + 2)

    def top_across(c, begin):
        part = top.at[c, :, begin:]
        return remote(part, part, top_pair.at[c], top_arrive.at[c], me, pair)

    def forward_top(c, begin):
        pl.when(has_next)(lambda: top_on(c, begin).start())
        pl.when(even)(lambda: top_across(c, begin).start())

    def forward_panel(c, h):
        pl.when(has_next)(lambda: panel_on(c, h).start())
        pl.when(even)(lambda: panel_across(c, h).start())

    def take_panel(c):
        for h in range(PARTS):
            panel_across(c, h).wait_recv()
            forward_panel(c, h)

    chained = has_next.astype(jnp.int32) + has_last.astype(jnp.int32)
    pl.semaphore_wait(barrier, log + 1 + chained)

    @pl.when(first)
    def _():
        def send(c, _):
            load_panel(c).wait()
            for h in range(PARTS):
                forward_panel(c, h)
            return 0

        lax.fori_loop(0, chunks, send, 0)

    size = stage.shape[1]
    pieces = depth // size

    def split_piece(piece, _):
        slot = piece % 2
        pl.when(piece + 1 < pieces)(lambda: load_stage(piece + 1, 1 - slot).start())
        load_stage(piece, slot).wait()
        for owner in range(n_obs):
            high, low = split(stage[slot, :, owner * rows : (owner + 1) * rows])
            where = pl.ds(pl.multiple_of(piece * size, size), size)
            high_part[owner, where, :] = high
            low_part[owner, where, :] = low
        return 0

    passes_on = jnp.logical_and(has_next, jnp.logical_not(first))
    lax.fori_loop(0, pieces // 2, split_piece, 0)
    pl.when(passes_on)(lambda: take_panel(0))
    lax.fori_loop(pieces // 2, pieces, split_piece, 0)

    def turn(level):
        mask = (1 - odd) * 2**level + odd * 2 ** (log - 1 - level)
        spacing = (1 - odd) * 2 ** (level + 1) + odd
        return mask, spacing

    def place(level, item):
        return n_obs - 2 ** (log - level) + item

    def sum_copy(c, level, item):
        mask, spacing = turn(level)
        at = place(level, item)
        return remote(
            sums.at[c, item * spacing + mask], landed.at[c, at],
            sum_send.at[c, at], sum_recv.at[c, at], flip(me, mask, log), unk,
        )

    def top_copy(c, level, begin):
        mask, _ = turn(level)
        return remote(
            top.at[c, :, begin:], top_landed.at[c, level, :, begin:],
            top_send.at[c, level], top_recv.at[c, level], flip(me, mask, log), unk,
        )

    def start_level(c, level):
        for item in range(2 ** (log - 1 - level)):
            sum_copy(c, level, item).start()
        pl.when(first)(lambda: in_group(c, lambda begin: top_copy(c, level, begin).start()))

    dot = functools.partial(jnp.dot, preferred_element_type=jnp.float32)

    def products(c):
        taken = jnp.logical_or(first, jnp.logical_and(passes_on, c == 0))
        pl.when(jnp.logical_not(taken))(lambda: take_panel(c))
        weighted = jnp.transpose(panels[c]) * weights_ref[...]
        high, low = split(weighted)
        both = jnp.concatenate([high, low], axis=0)

        def owner_block(q, _):
            owner = flip(me, q, log)
            wide = dot(both, high_part[owner])
            sums[c, q] = wide[:BLOCK] + wide[BLOCK:] + dot(high, low_part[owner])
            return 0

        lax.fori_loop(0, n_obs, owner_block, 0)

        @pl.when(first)
        def _():
            for owner in range(n_obs):
                start, stop = owner * real, min((owner + 1) * real, width)
                if start < stop:
                    top[c, :, start:stop] = sums[c, flip(me, owner, log), :, : stop - start]

        start_level(c, 0)

    def reduce_level(c, level):
        _, spacing = turn(level)
        for item in range(2 ** (log - 1 - level)):
            sum_copy(c, level, item).wait_recv()
            here = item * spacing
            sums[c, here] = sums[c, here] + landed[c, place(level, item)]

        @pl.when(first)
        def _():
            def add(begin):
                top_copy(c, level, begin).wait()
                top[c, :, begin:] = top[c, :, begin:] + top_landed[c, level, :, begin:]

            in_group(c, add)

        if level + 1 < log:
            start_level(c, level + 1)
        else:
            pl.when(first)(lambda: in_group(c, functools.partial(forward_top, c)))

    eye = (
        lax.broadcasted_iota(jnp.int32, (BLOCK, BLOCK), 0)
        == lax.broadcasted_iota(jnp.int32, (BLOCK, BLOCK), 1)
    ).astype(jnp.float32)

    def out_copy(c):
        return pltpu.make_async_copy(
            sums.at[c, 0],
            out_ref.at[pl.ds(pl.multiple_of(c * BLOCK, BLOCK), BLOCK), :],
            out_sem.at[c],
        )

    def factor(k):
        @pl.when(jnp.logical_not(first))
        def _():
            def arrive(begin):
                top_across(k, begin).wait_recv()
                forward_top(k, begin)

            in_group(k, arrive)

        offset = pl.multiple_of(k * BLOCK, BLOCK)

        def update(begin):
            block[:, begin:width] = top[k, :, begin:]
            block[:, width:] = sums[k, 0]

            def earlier(j, _):
                held = done[j, :, pl.ds(offset, BLOCK)]
                swapped = jnp.concatenate([held[BLOCK:], held[:BLOCK]], axis=0)
                block[:, begin:] = block[:, begin:] - (
                    dot_t(swapped, done[j, :, begin:])
                    + dot_t(held[:BLOCK], done[j, :BLOCK, begin:])
                )
                return 0

            lax.fori_loop(0, k, earlier, 0)

        in_group(k, update)
        work[:, :BLOCK] = block[:, pl.ds(offset, BLOCK)]
        work[:, BLOCK:] = eye
        invert_factor(work)

        def solve(begin):
            column = dot_3(work[:, BLOCK:], block[:, begin:])
            high, low = split(column)
            done[k, :BLOCK, begin:] = high
            done[k, BLOCK:, begin:] = low
            sums[k, 0] = column[:, width - begin :]

        in_group(k, solve)
        out_copy(k).start()

    def step(t, _):
        pl.when(t < chunks)(lambda: products(t))
        for level in range(log):
            c = t - 1 - level
            pl.when(jnp.logical_and(c >= 0, c < chunks))(functools.partial(reduce_level, c, level))
        pl.when(t >= log)(lambda: factor(t - log))
        return 0

    lax.fori_loop(0, chunks + log, step, 0)

    def drain(c, _):
        out_copy(c).wait()
        for level in range(log):
            for item in range(2 ** (log - 1 - level)):
                sum_copy(c, level, item).wait_send()

        @pl.when(has_next)
        def _():
            for h in range(PARTS):
                panel_on(c, h).wait_send()
            in_group(c, lambda begin: top_on(c, begin).wait_send())

        @pl.when(even)
        def _():
            for h in range(PARTS):
                panel_across(c, h).wait_send()
            in_group(c, lambda begin: top_across(c, begin).wait_send())

        return 0

    lax.fori_loop(0, chunks, drain, 0)


def fused(axes, real, panel, design, weights):
    n_obs, n_unk = axes
    log = n_obs.bit_length() - 1
    depth, columns = design.shape
    rows = columns // n_obs
    width = 2 * PANEL
    chunks = width // BLOCK
    piece = 64
    f32, bf16, dma = jnp.float32, jnp.bfloat16, pltpu.SemaphoreType.DMA
    return pl.pallas_call(
        functools.partial(fused_kernel, axes, log, real),
        out_shape=jax.ShapeDtypeStruct((width, rows), f32),
        in_specs=[
            pl.BlockSpec(memory_space=pl.ANY),
            pl.BlockSpec(memory_space=pl.ANY),
            pl.BlockSpec(memory_space=pltpu.VMEM),
        ],
        out_specs=pl.BlockSpec(memory_space=pl.ANY),
        scratch_shapes=[
            pltpu.VMEM((n_obs, depth, rows), bf16),
            pltpu.VMEM((n_obs, depth, rows), bf16),
            pltpu.VMEM((2, piece, columns), f32),
            pltpu.VMEM((chunks, depth, BLOCK), f32),
            pltpu.VMEM((chunks, n_obs, BLOCK, rows), f32),
            pltpu.VMEM((chunks, n_obs - 1, BLOCK, rows), f32),
            pltpu.VMEM((chunks, BLOCK, width), f32),
            pltpu.VMEM((chunks, log, BLOCK, width), f32),
            pltpu.VMEM((chunks, 2 * BLOCK, width + rows), bf16),
            pltpu.VMEM((BLOCK, 2 * BLOCK), f32),
            pltpu.VMEM((BLOCK, width + rows), f32),
            dma((2,)), dma((chunks,)),
            dma((chunks, PARTS)), dma((chunks, PARTS)), dma((chunks, PARTS)),
            dma((chunks, n_obs - 1)), dma((chunks, n_obs - 1)),
            dma((chunks, log)), dma((chunks, log)),
            dma((chunks,)), dma((chunks,)), dma((chunks,)), dma((chunks,)),
        ],
        compiler_params=pltpu.CompilerParams(
            collective_id=0, has_side_effects=True, vmem_limit_bytes=64 * 2**20 - 2**16
        ),
    )(panel, design, weights)


def local(axes, design, weights):
    n_obs, _ = axes
    depth, columns = design.shape
    rows = columns // n_obs
    padded = -(-rows // BLOCK) * BLOCK
    panel = design
    if padded != rows:
        design = jnp.pad(
            design.reshape(depth, n_obs, rows), ((0, 0), (0, 0), (0, padded - rows))
        ).reshape(depth, n_obs * padded)
    return fused(axes, rows, panel, design, weights[None, :])[:, :rows].T


def solution(mesh):
    axes = (mesh.shape["obs"], mesh.shape["unk"])
    return jax.shard_map(
        functools.partial(local, axes),
        mesh=mesh,
        in_specs=(P("obs", "unk"), P("obs")),
        out_specs=P(("unk", "obs"), None),
        check_vma=False,
    )
```
